32 devices in a mesh: outer: 4 (over x, core), dp: 8 (over z, y).
Axes of the slice: x: 2, y: 2, z: 4, core: 2. Of those that a mesh axis runs over, the one named last changes fastest.
Arguments:
- query_ids: int32 [32, 512], P(('outer', 'dp')), may hold values from 0 to 30521
- query_mask: int32 [32, 512], P(('outer', 'dp')), may hold values from 0 to 1, as said below
- passage_ids: int32 [32, 512], P(('outer', 'dp')), may hold values from 0 to 30521
- passage_mask: int32 [32, 512], P(('outer', 'dp')), may hold values from 0 to 1, as said below
- source: int32 [32], replicated, may hold values from 0 to 3
- positive: int32 [32], replicated, may hold values from 0 to 31, each once
- table: float32 [30720, 768], P(('outer', 'dp')), may hold values from -0.3125 to 0.3125
- positions: float32 [512, 768], P(('outer', 'dp')), may hold values from -0.3125 to 0.3125
- w_qkv: float32 [768, 2304], P(('outer', 'dp')), may hold values from -0.21875 to 0.21875
- w_o: float32 [768, 768], P(('outer', 'dp')), may hold values from -0.875 to 0.875
- w_in: float32 [768, 3072], P(('outer', 'dp')), may hold values from -0.21875 to 0.21875
- w_out: float32 [3072, 768], P(('outer', 'dp')), may hold values from -0.109375 to 0.109375
- vectors: float32 [14, 768], P(None, ('outer', 'dp')), may hold values from -0.4 to 1.4, as said below
- first_table: float32 [30720, 768], P(('outer', 'dp')), may hold values from -5.722046e-06 to 5.722046e-06
- first_positions: float32 [512, 768], P(('outer', 'dp')), may hold values from -5.722046e-06 to 5.722046e-06
- first_qkv: float32 [768, 2304], P(('outer', 'dp')), may hold values from -5.722046e-06 to 5.722046e-06
- first_o: float32 [768, 768], P(('outer', 'dp')), may hold values from -5.722046e-06 to 5.722046e-06
- first_in: float32 [768, 3072], P(('outer', 'dp')), may hold values from -5.722046e-06 to 5.722046e-06
- first_out: float32 [3072, 768], P(('outer', 'dp')), may hold values from -5.722046e-06 to 5.722046e-06
- first_vectors: float32 [14, 768], P(None, ('outer', 'dp')), may hold values from -3.0517578e-05 to 3.0517578e-05
- second_table: float32 [30720, 768], P(('outer', 'dp')), may hold values from 1.60902e-12 to 6.43608e-12
- second_positions: float32 [512, 768], P(('outer', 'dp')), may hold values from 8.0451e-14 to 3.21804e-13
- second_qkv: float32 [768, 2304], P(('outer', 'dp')), may hold values from 8.0451e-14 to 3.21804e-13
- second_o: float32 [768, 768], P(('outer', 'dp')), may hold values from 8.0451e-14 to 3.21804e-13
- second_in: float32 [768, 3072], P(('outer', 'dp')), may hold values from 8.0451e-14 to 3.21804e-13
- second_out: float32 [3072, 768], P(('outer', 'dp')), may hold values from 8.0451e-14 to 3.21804e-13
- second_vectors: float32 [14, 768], P(None, ('outer', 'dp')), may hold values from 2.011275e-12 to 8.0451e-12
Outputs:
- new_table: float32 [30720, 768], P(('outer', 'dp'))
- new_positions: float32 [512, 768], P(('outer', 'dp'))
- new_qkv: float32 [768, 2304], P(('outer', 'dp'))
- new_o: float32 [768, 768], P(('outer', 'dp'))
- new_in: float32 [768, 3072], P(('outer', 'dp'))
- new_out: float32 [3072, 768], P(('outer', 'dp'))
- new_vectors: float32 [14, 768], P(None, ('outer', 'dp'))
- moment_table: float32 [30720, 768], P(('outer', 'dp'))
- moment_positions: float32 [512, 768], P(('outer', 'dp'))
- moment_qkv: float32 [768, 2304], P(('outer', 'dp'))
- moment_o: float32 [768, 768], P(('outer', 'dp'))
- moment_in: float32 [768, 3072], P(('outer', 'dp'))
- moment_out: float32 [3072, 768], P(('outer', 'dp'))
- moment_vectors: float32 [14, 768], P(None, ('outer', 'dp'))
- square_table: float32 [30720, 768], P(('outer', 'dp'))
- square_positions: float32 [512, 768], P(('outer', 'dp'))
- square_qkv: float32 [768, 2304], P(('outer', 'dp'))
- square_o: float32 [768, 768], P(('outer', 'dp'))
- square_in: float32 [768, 3072], P(('outer', 'dp'))
- square_out: float32 [3072, 768], P(('outer', 'dp'))
- square_vectors: float32 [14, 768], P(None, ('outer', 'dp'))
- loss: float32 [], replicated
- grad_norm: float32 [], replicated
The draws below stay inside these ranges and needn't reach their ends.
Inputs may be any that keep to these rules, and one draw needn't show every extreme that they name: `query_mask`: each row is 1 on a prefix of 64 or more positions and 0 after it. `passage_mask`: each row is 1 on a prefix of 128 or more positions and 0 after it. `vectors`: rows 8, 10, 12 lie within 0.6 to 1.4, the others within -0.4 to 0.4.
All inputs are finite; a program needn't handle non-finite values.
Results may differ from the reference program's by a relative error of at most 0.012.
The reference program's roundings to bfloat16 on the way count: a program that leaves them out, or rounds other values in their place, can miss the bound.
Values may be sent and summed in bfloat16 or wider, within the bound.
No kernel may reach another device: no remote copies, remote signals or barrier semaphores. Data moves between devices by JAX's collectives and lax.ppermute only.
A program may use at most 320 MiB of HBM per device.

```python
import math
import jax
import jax.numpy as jnp
import numpy as np
from jax import lax

D = 768
HEADS = 12
HEAD_DIM = 64
FF = 3072
VOCAB = 30522
POS = 512
ROWS_EMB = 30720
M1 = 64
M2 = 128
M3 = 256
L = 512
SOURCES = 4
STEP = 10
PAIRS = 32
NPARAM = 31074816


def prefix_mask(key, shortest):
    lengths = jax.random.randint(key, (PAIRS, 1), shortest, L + 1)
    return (jnp.arange(L)[None, :] < lengths).astype(jnp.int32)


def draw_query_mask(key, part):
    key = jax.random.fold_in(key, 11)
    return prefix_mask(key, L // 8)


def draw_passage_mask(key, part):
    key = jax.random.fold_in(key, 12)
    return prefix_mask(key, L // 4)


def draw_vectors(key, part):
    key = jax.random.fold_in(key, 13)
    rows = jnp.clip(jax.random.normal(key, (14, D), jnp.float32) * 0.1, -0.4, 0.4)
    gains = jnp.zeros((14, 1), jnp.float32).at[jnp.array([8, 10, 12])].set(1.0)
    return rows + gains


def with_ends(drawn, stream_key, least, top_value):
    extent = drawn.shape
    place = [jax.random.randint(jax.random.fold_in(stream_key, axis), (), 0, extent[axis]) for axis in range(len(extent))]
    drawn = drawn.at[tuple(place)].set(least)
    longest = extent.index(max(extent))
    place[longest] = (place[longest] + 1) % extent[longest]
    return drawn.at[tuple(place)].set(top_value)


def shard_levels(key, shape, pieces, smallest, top_value):
    loudness, own = 1.0, jax.random.fold_in(key, 6)
    for position, blocks in pieces:
        heights = jnp.exp(jax.random.uniform(jax.random.fold_in(own, position), (blocks,), jnp.float32, smallest / len(pieces), top_value / len(pieces)))
        loudness = loudness * jnp.repeat(heights, shape[position] // blocks).reshape([-1 if axis == position else 1 for axis in range(len(shape))])
    return loudness


def rank_table(number_of, lean):
    weights = [(1 << 20) // math.isqrt(rank ** lean) + 1 for rank in range(1, number_of + 1)]
    scale = 1 + sum(weights) // (1 << 30)
    return np.cumsum(np.array([max(1, weight // scale) for weight in weights]))


def ranked_ids(stream_key, shape, count, slope):
    table = rank_table(count, slope)
    lot = jax.random.randint(jax.random.fold_in(stream_key, 1), shape, 0, int(table[count - 1]))
    standing = jnp.searchsorted(jnp.asarray(table, jnp.int32), lot, side="right")
    return jax.random.permutation(jax.random.fold_in(stream_key, 2), count)[standing].astype(jnp.int32)


def scatter_about(rng, shape, scale, most, cuts=(), held_as=jnp.bfloat16):
    gain = shard_levels(rng, shape, cuts, -0.22, 0.18) if cuts else 1.0
    values = jax.random.normal(rng, shape, jnp.float32) * scale * gain
    return jnp.minimum(jnp.maximum(values, -most), most).astype(held_as)


def setup_inputs(seed: int = 0) -> dict:
    streams_of = jax.random.split(jax.random.key(seed), 28)
    query_ids = with_ends(ranked_ids(streams_of[0], (PAIRS, L), VOCAB, 2), jax.random.fold_in(streams_of[0], 3), 0, VOCAB - 1).astype(jnp.int32)
    query_mask = draw_query_mask(jax.random.fold_in(streams_of[27], 71), 0)
    passage_ids = with_ends(ranked_ids(streams_of[2], (PAIRS, L), VOCAB, 2), jax.random.fold_in(streams_of[2], 3), 0, VOCAB - 1).astype(jnp.int32)
    passage_mask = draw_passage_mask(jax.random.fold_in(streams_of[27], 71), 0)
    source = with_ends(jax.random.randint(streams_of[4], (PAIRS,), 0, SOURCES), jax.random.fold_in(streams_of[4], 1), 0, SOURCES - 1).astype(jnp.int32)
    positive = jax.random.permutation(streams_of[5], PAIRS).astype(jnp.int32)
    table = scatter_about(streams_of[6], (ROWS_EMB, D), 0.05, 0.3125, ((0, 32),), jnp.float32)
    positions = scatter_about(streams_of[7], (POS, D), 0.05, 0.3125, ((0, 32),), jnp.float32)
    w_qkv = scatter_about(streams_of[8], (D, 3 * D), D ** -0.5, 0.21875, ((0, 32),), jnp.float32)
    w_o = scatter_about(streams_of[9], (D, D), (D * 32 // L) ** -0.5, 0.875, ((0, 32),), jnp.float32)
    w_in = scatter_about(streams_of[10], (D, FF), D ** -0.5, 0.21875, ((0, 32),), jnp.float32)
    w_out = scatter_about(streams_of[11], (FF, D), FF ** -0.5, 0.109375, ((0, 32),), jnp.float32)
    vectors = draw_vectors(jax.random.fold_in(streams_of[27], 71), 0)
    first_table = scatter_about(streams_of[13], (ROWS_EMB, D), (0.0055 * NPARAM ** -0.5), 5.7220458984375e-06, ((0, 32),), jnp.float32)
    first_positions = scatter_about(streams_of[14], (POS, D), (0.0055 * NPARAM ** -0.5), 5.7220458984375e-06, ((0, 32),), jnp.float32)
    first_qkv = scatter_about(streams_of[15], (D, 3 * D), (0.0055 * NPARAM ** -0.5), 5.7220458984375e-06, ((0, 32),), jnp.float32)
    first_o = scatter_about(streams_of[16], (D, D), (0.0055 * NPARAM ** -0.5), 5.7220458984375e-06, ((0, 32),), jnp.float32)
    first_in = scatter_about(streams_of[17], (D, FF), (0.0055 * NPARAM ** -0.5), 5.7220458984375e-06, ((0, 32),), jnp.float32)
    first_out = scatter_about(streams_of[18], (FF, D), (0.0055 * NPARAM ** -0.5), 5.7220458984375e-06, ((0, 32),), jnp.float32)
    first_vectors = scatter_about(streams_of[19], (14, D), (0.0275 * NPARAM ** -0.5), 3.0517578125e-05, ((1, 32),), jnp.float32)
    second_table = jnp.clip(jnp.exp(math.log(6.436079967586661e-12) - 1.3862944 * jax.random.uniform(streams_of[20], (ROWS_EMB, D), jnp.float32) ** shard_levels(streams_of[20], (ROWS_EMB, D), ((0, 32),), -0.2, 0.2)), 1.6090199918966652e-12, 6.436079967586661e-12)
    second_positions = jnp.clip(jnp.exp(math.log(3.2180399837933304e-13) - 1.3862944 * jax.random.uniform(streams_of[21], (POS, D), jnp.float32) ** shard_levels(streams_of[21], (POS, D), ((0, 32),), -0.2, 0.2)), 8.045099959483326e-14, 3.2180399837933304e-13)
    second_qkv = jnp.clip(jnp.exp(math.log(3.2180399837933304e-13) - 1.3862944 * jax.random.uniform(streams_of[22], (D, 3 * D), jnp.float32) ** shard_levels(streams_of[22], (D, 3 * D), ((0, 32),), -0.2, 0.2)), 8.045099959483326e-14, 3.2180399837933304e-13)
    second_o = jnp.clip(jnp.exp(math.log(3.2180399837933304e-13) - 1.3862944 * jax.random.uniform(streams_of[23], (D, D), jnp.float32) ** shard_levels(streams_of[23], (D, D), ((0, 32),), -0.2, 0.2)), 8.045099959483326e-14, 3.2180399837933304e-13)
    second_in = jnp.clip(jnp.exp(math.log(3.2180399837933304e-13) - 1.3862944 * jax.random.uniform(streams_of[24], (D, FF), jnp.float32) ** shard_levels(streams_of[24], (D, FF), ((0, 32),), -0.2, 0.2)), 8.045099959483326e-14, 3.2180399837933304e-13)
    second_out = jnp.clip(jnp.exp(math.log(3.2180399837933304e-13) - 1.3862944 * jax.random.uniform(streams_of[25], (FF, D), jnp.float32) ** shard_levels(streams_of[25], (FF, D), ((0, 32),), -0.2, 0.2)), 8.045099959483326e-14, 3.2180399837933304e-13)
    second_vectors = jnp.clip(jnp.exp(math.log(8.04510017632376e-12) - 1.3862944 * jax.random.uniform(streams_of[26], (14, D), jnp.float32) ** shard_levels(streams_of[26], (14, D), ((1, 32),), -0.2, 0.2)), 2.01127504408094e-12, 8.04510017632376e-12)
    return dict(query_ids=query_ids, query_mask=query_mask, passage_ids=passage_ids, passage_mask=passage_mask, source=source, positive=positive, table=table, positions=positions, w_qkv=w_qkv, w_o=w_o, w_in=w_in, w_out=w_out, vectors=vectors, first_table=first_table, first_positions=first_positions, first_qkv=first_qkv, first_o=first_o, first_in=first_in, first_out=first_out, first_vectors=first_vectors, second_table=second_table, second_positions=second_positions, second_qkv=second_qkv, second_o=second_o, second_in=second_in, second_out=second_out, second_vectors=second_vectors)


TEMPER = 0.01
CLIP_LIMIT = 0.05
LEARN_RATE = 0.1
VECTOR_RATE = 0.3
BETA_FIRST = 0.9
BETA_SECOND = 0.999
WEIGHT_DECAY = 0.01
EPSILON = 1e-08
NORM_EPSILON = 1e-12
PRECISE = lax.Precision.HIGHEST

@jax.custom_vjp
def low(v):
    return lax.optimization_barrier(v.astype(jnp.bfloat16)).astype(jnp.float32)

@jax.custom_vjp
def low_back(v):
    return v

def low_keep(v):
    return (low(v), None)

def low_pass(kept, grad):
    return (grad,)

def back_keep(v):
    return (v, None)

def back_low(kept, grad):
    return (low(grad),)
low.defvjp(low_keep, low_pass)
low_back.defvjp(back_keep, back_low)

def layer_norm(values, gain_row, shift_row):
    centre = values - lax.optimization_barrier(jnp.mean(values, -1, keepdims=True))
    spread = lax.optimization_barrier(jnp.mean(centre * centre, -1, keepdims=True))
    return centre * lax.rsqrt(spread + NORM_EPSILON) * gain_row + shift_row

def project(values, matrix):
    return jnp.einsum('gld,de->gle', values, matrix, precision=PRECISE)

def encode(weights, token_ids, token_mask):
    table, positions, w_qkv, w_o, w_in, w_out, vectors = weights
    groups, length = token_ids.shape
    embedded = jnp.take(table, token_ids, axis=0) + positions[:length][None]
    hidden_zero = layer_norm(embedded, vectors[8], vectors[9])
    bias_qkv = jnp.concatenate([vectors[0], jnp.zeros_like(vectors[0]), vectors[1]])
    packed = low(low_back(project(low(hidden_zero), w_qkv) + bias_qkv))
    packed = packed.reshape(groups, length, 3, HEADS, HEAD_DIM)
    scores = jnp.einsum('gqhc,gkhc->ghqk', packed[:, :, 0], packed[:, :, 1], precision=PRECISE) * HEAD_DIM ** (-0.5)
    keeping = token_mask[:, None, None, :] > 0
    scores = low_back(jnp.where(keeping, scores, -1000000000.0))
    attn_weights = jax.nn.softmax(scores, -1)
    context = jnp.einsum('ghqk,gkhc->gqhc', low(attn_weights), packed[:, :, 2], precision=PRECISE)
    context = low(low_back(context)).reshape(groups, length, D)
    attended = low_back(project(context, w_o) + vectors[2])
    hidden_one = layer_norm(hidden_zero + attended, vectors[10], vectors[11])
    inner_pre = low_back(project(low(hidden_one), w_in) + vectors[3:7].reshape(-1))
    activated = low(jax.nn.gelu(inner_pre, approximate=False))
    branch_out = low_back(project(activated, w_out) + vectors[7])
    hidden_two = layer_norm(hidden_one + branch_out, vectors[12], vectors[13])
    weight_mask = token_mask.astype(jnp.float32)
    pooled = lax.optimization_barrier(jnp.sum(hidden_two * weight_mask[:, :, None], 1)) / lax.optimization_barrier(jnp.sum(weight_mask, 1))[:, None]
    return pooled * lax.rsqrt(lax.optimization_barrier(jnp.sum(pooled * pooled, -1, keepdims=True)) + NORM_EPSILON)

def info_loss(queries, passages, query_rows, source, positive):
    own_positive = jnp.take(positive, query_rows)
    keeping = source[None, :] == jnp.take(source, own_positive)[:, None]
    total = jnp.zeros((), jnp.float32)
    for nested in (M1, M2, M3, D):
        left = queries[:, :nested]
        left = left * lax.rsqrt(lax.optimization_barrier(jnp.sum(left * left, -1, keepdims=True)) + NORM_EPSILON)
        right = passages[:, :nested]
        right = right * lax.rsqrt(lax.optimization_barrier(jnp.sum(right * right, -1, keepdims=True)) + NORM_EPSILON)
        scores = jnp.dot(left, right.T, precision=PRECISE) / TEMPER
        scores = jnp.where(keeping, scores, -1000000000.0)
        row_peak = lax.optimization_barrier(jnp.max(scores, -1, keepdims=True))
        log_total = row_peak[:, 0] + jnp.log(lax.optimization_barrier(jnp.sum(jnp.exp(scores - row_peak), -1)))
        target = jnp.take_along_axis(scores, own_positive[:, None], 1)[:, 0]
        total = total + jnp.sum(log_total - target)
    return total / passages.shape[0]

def reference(query_ids, query_mask, passage_ids, passage_mask, source, positive, table, positions, w_qkv, w_o, w_in, w_out, vectors, first_table, first_positions, first_qkv, first_o, first_in, first_out, first_vectors, second_table, second_positions, second_qkv, second_o, second_in, second_out, second_vectors):
    masters = (table, positions, w_qkv, w_o, w_in, w_out, vectors)
    firsts = (first_table, first_positions, first_qkv, first_o, first_in, first_out, first_vectors)
    seconds = (second_table, second_positions, second_qkv, second_o, second_in, second_out, second_vectors)

    def objective(params):
        weights = tuple((low(param) for param in params))

        def encode_group(pair):
            return jax.checkpoint(encode)(weights, pair[0], pair[1])

        def encode_all(token_ids, token_mask):
            result = lax.map(encode_group, (token_ids.reshape(-1, 8, L), token_mask.reshape(-1, 8, L)))
            return result.reshape(-1, D)
        queries = encode_all(query_ids, query_mask)
        passages = encode_all(passage_ids, passage_mask)
        return info_loss(queries, passages, jnp.arange(PAIRS, dtype=jnp.int32), source, positive)
    loss, pullback = jax.vjp(objective, masters)
    gradients = pullback(jnp.ones((), jnp.float32))[0]
    squares = jnp.zeros((), jnp.float32)
    for gradient in gradients:
        squares = squares + jnp.sum(gradient * gradient)
    grad_norm = jnp.sqrt(squares)
    factor = jnp.minimum(1.0, CLIP_LIMIT / (grad_norm + 1e-06))
    rates = (LEARN_RATE,) * 6 + (VECTOR_RATE,)
    decays = (WEIGHT_DECAY,) * 6 + (0.0,)
    new_masters, new_firsts, new_seconds = ([], [], [])
    for master, first, second, gradient, rate, decay in zip(masters, firsts, seconds, gradients, rates, decays):
        clipped = gradient * factor
        first = BETA_FIRST * first + (1.0 - BETA_FIRST) * clipped
        second = BETA_SECOND * second + (1.0 - BETA_SECOND) * clipped * clipped
        ratio = first / (1.0 - BETA_FIRST ** STEP) / (jnp.sqrt(second / (1.0 - BETA_SECOND ** STEP)) + EPSILON)
        new_masters.append(master - rate * (ratio + decay * master))
        new_firsts.append(first)
        new_seconds.append(second)
    return (new_masters[0], new_masters[1], new_masters[2], new_masters[3], new_masters[4], new_masters[5], new_masters[6], new_firsts[0], new_firsts[1], new_firsts[2], new_firsts[3], new_firsts[4], new_firsts[5], new_firsts[6], new_seconds[0], new_seconds[1], new_seconds[2], new_seconds[3], new_seconds[4], new_seconds[5], new_seconds[6], loss, grad_norm)
```

```python
import functools

import jax
import jax.numpy as jnp
import numpy as np
from jax import lax
from jax.experimental import pallas as pl
from jax.experimental.pallas import tpu as pltpu
from jax.sharding import Mesh, PartitionSpec as P

D = 768
HEADS = 12
HEAD_DIM = 64
WIDTHS = (64, 128, 256, 768)
STEP = 10
TEMPER = 0.01
CLIP_LIMIT = 0.05
LEARN_RATE = 0.1
VECTOR_RATE = 0.3
BETA_FIRST = 0.9
BETA_SECOND = 0.999
WEIGHT_DECAY = 0.01
EPSILON = 1e-08
NORM_EPSILON = 1e-12
F32 = jnp.float32
BF16 = jnp.bfloat16
AXES = ("x", "core", "z", "y")
LANES = 128
MIB = 1024 * 1024


def matmul(left, right):
    return jnp.dot(left, right, preferred_element_type=F32)


def contract(left, right, left_dim, right_dim, precision=None):
    return lax.dot_general(
        left, right, (((left_dim,), (right_dim,)), ((), ())),
        precision=precision, preferred_element_type=F32,
    )


CHEAP = pl.CostEstimate(flops=1, bytes_accessed=1, transcendentals=0)
BLOCK = 256


def round_up(value, multiple):
    return -(-value // multiple) * multiple


def normalize(values):
    centre = values - jnp.mean(values, -1, keepdims=True)
    scale = lax.rsqrt(jnp.mean(centre * centre, -1, keepdims=True) + NORM_EPSILON)
    return centre * scale, scale


def normalize_back(grad_out, gain_row, normal, scale):
    grad = grad_out * gain_row
    return scale * (
        grad
        - jnp.mean(grad, -1, keepdims=True)
        - normal * jnp.mean(grad * normal, -1, keepdims=True)
    )


def column_sum(values):
    return jnp.sum(values, 0, keepdims=True)


def row_blocks(width, offset=0):
    return pl.BlockSpec((BLOCK, width), lambda i: (i, offset))


def fixed(shape, *index):
    index = index or (0,) * len(shape)
    return pl.BlockSpec(shape, lambda i: index, pipeline_mode=pl.Buffered(1))


def weight_blocks(first, count):
    return [fixed((D, D), 0, first + part) for part in range(count)]


def weight_row_blocks(count):
    return [fixed((D, D), part, 0) for part in range(count)]


ROOMY = ("update", "finish", "pieces", "lookup", "assemble", "assemble_pair", "grad_packed", "layer_back", "layer", "split_packed", "enter", "vec",)


def call(kernel, name, grid, in_specs, out_specs, out_shape, scratch=(), vmem=36):
    vmem = 60 if name in ROOMY else vmem
    return pl.pallas_call(
        kernel,
        grid=grid,
        in_specs=in_specs,
        out_specs=out_specs,
        out_shape=out_shape,
        scratch_shapes=scratch,
        cost_estimate=CHEAP,
        compiler_params=pltpu.CompilerParams(vmem_limit_bytes=vmem * MIB),
        name=name,
    )


def shape(rows, width, dtype):
    return jax.ShapeDtypeStruct((rows, width), dtype)


def pair_kernel(w_in, w_out, out_ref):
    pieces, rows = out_ref.shape[0] // 2, out_ref.shape[1]
    for piece in range(pieces):
        out_ref[piece] = w_in[:, piece * D : (piece + 1) * D].astype(BF16)
        out_ref[pieces + piece] = w_out[piece * rows : (piece + 1) * rows].astype(BF16)


def pair_of(w_in, w_out):
    rows, pieces = w_in.shape[0], w_in.shape[1] // D
    return call(
        pair_kernel, "pair", (1,), [fixed(w_in.shape), fixed(w_out.shape)], fixed((2 * pieces, rows, D)),
        jax.ShapeDtypeStruct((2 * pieces, rows, D), BF16),
    )(w_in, w_out)


def pieces_kernel(w_qkv, w_o, positions, vectors, w_in, w_out, out_ref):
    rows = out_ref.shape[1]
    small = [positions[...], vectors[...]]
    rest = rows - sum(part.shape[0] for part in small)
    if rest:
        small.append(jnp.zeros((rest, D), F32))
    parts = [w_qkv[:, piece * D : (piece + 1) * D] for piece in range(3)]
    parts += [w_o[...], jnp.concatenate(small, 0)]
    parts += [w_in[:, first : first + D] for first in range(0, w_in.shape[1], D)]
    parts += [w_out[first : first + rows] for first in range(0, w_out.shape[0], rows)]
    for piece, part in enumerate(parts):
        out_ref[piece] = part.astype(BF16)


def pieces_of(*parts):
    rows = parts[0].shape[0]
    extent = (5 + parts[4].shape[1] // D + parts[5].shape[0] // rows, rows, D)
    return call(
        pieces_kernel, "pieces", (1,), [fixed(part.shape) for part in parts], fixed(extent),
        jax.ShapeDtypeStruct(extent, BF16),
    )(*parts)


def vec_kernel(skip, width, rows, small, vec_ref):
    index = lambda axis: lax.broadcasted_iota(jnp.int32, (D, D), axis)
    mark = lambda chosen: jnp.where(chosen, 1.0, 0.0).astype(BF16)
    spot, column = index(0), index(1)
    held = matmul(mark(column == spot // width * rows + skip), small[...])
    held = jnp.where(column % width == spot % width, held, 0.0).astype(BF16)
    lanes = lax.broadcasted_iota(jnp.int32, (D, LANES), 1)
    part = lax.broadcasted_iota(jnp.int32, (D, LANES), 0) // width
    vec_ref[...] = matmul(held, mark(part == lanes)).T[: vec_ref.shape[0]]


def vec_of(gathered, count, width, skip, rows):
    return call(
        functools.partial(vec_kernel, skip, width, rows), "vec", (1,),
        [pl.BlockSpec((D, D), lambda i: (0, 4))], fixed((round_up(count, 8), D)),
        shape(round_up(count, 8), D, F32),
    )(gathered)


def plan_kernel(owned, room, query_ids, passage_ids, slot_column, slot_row, rank_row, fresh_row, wanted):
    tokens = slot_row.shape[1]
    row = [ref[index : index + 1, :] for ref in (query_ids, passage_ids) for index in range(ref.shape[0])]
    row = jnp.concatenate(row, 1)
    column = jnp.broadcast_to(row.astype(F32), (8, tokens)).T[:, :1].astype(jnp.int32)
    down = lax.broadcasted_iota(jnp.int32, (tokens, tokens), 0)
    across = lax.broadcasted_iota(jnp.int32, (tokens, tokens), 1)
    count = lambda chosen, axis: jnp.sum(jnp.where(chosen, 1, 0), axis, keepdims=True)
    equal = column == row
    new_column = count(equal & (across < down), 1) == 0
    new_row = count(equal & (down < across), 0) == 0
    holder_column, holder_row = column // owned, row // owned
    together = holder_column == holder_row
    rank_of_column = count(together & (row < column) & new_row, 1)
    rank_of_row = count(together & (column < row) & new_column, 0)
    slot = lambda holder, rank: jnp.where(rank < room - 1, holder * room + rank, -1)
    slot_column[...] = slot(holder_column, rank_of_column)
    slot_row[...] = slot(holder_row, rank_of_row)
    rank_row[...] = rank_of_row
    fresh_row[...] = jnp.where(new_row, 1, 0)
    devices = wanted.shape[0]
    mine = (lax.broadcasted_iota(jnp.int32, (devices, tokens), 0) == holder_row) & new_row
    lanes = lax.broadcasted_iota(jnp.int32, (tokens, LANES), 1)
    spots = jnp.where((rank_of_column == lanes) & (lanes < room - 1), 1.0, 0.0).astype(BF16)
    ask = row - holder_row * owned + 1
    high = ask // 64
    pick = lambda values: matmul(jnp.where(mine, values, 0).astype(F32).astype(BF16), spots)
    asks = pick(high) * 64.0 + pick(ask - high * 64)
    deepest = jnp.max(rank_of_row, 1, keepdims=True)
    lanes = lax.broadcasted_iota(jnp.int32, (devices, LANES), 1)
    wanted[...] = jnp.where(lanes == LANES - 1, deepest, asks.astype(jnp.int32))


def plan_of(query_ids, passage_ids, owned, room, devices):
    tokens = query_ids.size + passage_ids.size
    ints = lambda *extent: jax.ShapeDtypeStruct(extent, jnp.int32)
    row = fixed((1, tokens))
    return call(
        functools.partial(plan_kernel, owned, room), "plan", (1,),
        [fixed(query_ids.shape), fixed(passage_ids.shape)],
        [fixed((tokens, 1)), row, row, row, fixed((devices, LANES))],
        [ints(tokens, 1), ints(1, tokens), ints(1, tokens), ints(1, tokens), ints(devices, LANES)],
    )(query_ids, passage_ids)


def lookup_kernel(room, asked, table, chosen_ref, found_ref):
    asks = asked[...].astype(F32).T
    devices, owned = asked.shape[0], table.shape[0]
    rows = lax.broadcasted_iota(jnp.int32, (room, owned), 1).astype(F32) + 1.0
    for device in range(0, devices, 2):
        both = [jnp.where(asks[:room, side : side + 1] == rows, 1.0, 0.0) for side in (device, device + 1)]
        chosen_ref[device * room : (device + 2) * room] = jnp.concatenate(both, 0).astype(BF16)
    found_ref[...] = matmul(chosen_ref[...], table[...].astype(BF16)).astype(BF16)


def lookup(asked, table, room):
    slots = asked.shape[0] * room
    owned = table.shape[0]
    return call(
        functools.partial(lookup_kernel, room), "lookup", (1,),
        [fixed(asked.shape), fixed(table.shape)],
        [fixed((slots, owned)), fixed((slots, D))],
        [shape(slots, owned, BF16), shape(slots, D, BF16)],
    )(asked, table)


def take_kernel(chosen, given, grad_ref):
    grad_ref[...] = contract(chosen[...], given[...], 0, 0)


def take_rows(chosen, given):
    owned = chosen.shape[1]
    return call(
        take_kernel, "take", (1,), [fixed(chosen.shape), fixed(given.shape)], fixed((owned, D)),
        shape(owned, D, F32),
    )(chosen, given)


def enter_kernel(place_rows, rows, slot_ref, found_ref, x_ref, place_ref, vec_ref, wq_ref, wk_ref, wv_ref, normal_ref, scale_ref, low_ref, packed_ref):
    places = place_ref[...].astype(F32)
    places = [places[first : first + place_rows] for first in range(0, places.shape[0], rows)]
    places = jnp.concatenate(places, 0) + x_ref[...]
    slots = lax.broadcasted_iota(jnp.int32, (BLOCK, found_ref.shape[0]), 1)
    chosen = jnp.where(slot_ref[...] == slots, 1.0, 0.0).astype(BF16)
    normal, scale = normalize(matmul(chosen, found_ref[...]) + places)
    low = (normal * vec_ref[8:9] + vec_ref[9:10]).astype(BF16)
    normal_ref[...], scale_ref[...], low_ref[...] = normal, scale, low
    for part, (weight, bias) in enumerate(((wq_ref, 0), (wk_ref, None), (wv_ref, 1))):
        out = matmul(low, weight[...])
        if bias is not None:
            out = out + vec_ref[bias : bias + 1]
        packed_ref[:, part * D : (part + 1) * D] = out.astype(BF16)


def enter(slot, found, looked_up, vec, gathered, length, place_rows, rows):
    tokens = looked_up.shape[0]
    cycle = length // BLOCK
    place_block = pl.BlockSpec((BLOCK // place_rows * rows, D), lambda i: (i % cycle, 4))
    return call(
        functools.partial(enter_kernel, place_rows, rows), "enter", (tokens // BLOCK,),
        [row_blocks(1), fixed(found.shape), row_blocks(D), place_block, fixed(vec.shape)]
        + weight_blocks(0, 3),
        [row_blocks(D), row_blocks(1), row_blocks(D), row_blocks(3 * D)],
        [shape(tokens, D, F32), shape(tokens, 1, F32), shape(tokens, D, BF16), shape(tokens, 3 * D, BF16)],
    )(slot, found, looked_up, gathered, vec, *[gathered] * 3)


def layer_kernel(cycle, pieces, *refs):
    normal_zero, context, share, vec, w_o = refs[:5]
    w_in, w_out = refs[5 : 5 + pieces], refs[5 + pieces : 5 + 2 * pieces]
    normal_one_ref, scale_one_ref, low_one_ref, active_ref, slope_ref = refs[5 + 2 * pieces : 10 + 2 * pieces]
    normal_two_ref, scale_two_ref, pooled_ref = refs[10 + 2 * pieces :]
    hidden = normal_zero[...] * vec[8:9] + vec[9:10]
    normal_one, scale_one = normalize(hidden + matmul(context[...], w_o[...]) + vec[2:3])
    hidden = normal_one * vec[10:11] + vec[11:12]
    low = hidden.astype(BF16)
    normal_one_ref[...], scale_one_ref[...], low_one_ref[...] = normal_one, scale_one, low
    total = hidden + vec[7:8]
    for part in range(pieces):
        columns = slice(part * D, (part + 1) * D)
        inner = matmul(low, w_in[part][...]) + vec[3 + part : 4 + part]
        gate = 0.5 + 0.5 * lax.erf(inner * (0.5**0.5))
        active = (inner * gate).astype(BF16)
        active_ref[:, columns] = active
        slope_ref[:, columns] = gate + inner * jnp.exp(-0.5 * inner * inner) * (2.0 * np.pi) ** -0.5
        total = total + matmul(active, w_out[part][...])
    normal_two, scale_two = normalize(total)
    normal_two_ref[...], scale_two_ref[...] = normal_two, scale_two
    pooled = column_sum((normal_two * vec[12:13] + vec[13:14]) * share[...])

    @pl.when(pl.program_id(0) % cycle == 0)
    def _():
        pooled_ref[0] = jnp.zeros((1, D), F32)

    pooled_ref[0] += pooled


def layer(normal_zero, context, share, vec, gathered, w_in, w_out, length):
    tokens, units = normal_zero.shape[0], w_in.shape[1]
    cycle, pieces = length // BLOCK, units // D
    return call(
        functools.partial(layer_kernel, cycle, pieces), "layer", (tokens // BLOCK,),
        [row_blocks(D), row_blocks(D), row_blocks(1), fixed(vec.shape)]
        + weight_blocks(3, 1) + weight_blocks(0, pieces) + weight_row_blocks(pieces),
        [row_blocks(D), row_blocks(1), row_blocks(D), row_blocks(units), row_blocks(units)]
        + [row_blocks(D), row_blocks(1), pl.BlockSpec((1, 1, D), lambda i: (i // cycle, 0, 0))],
        [shape(tokens, D, F32), shape(tokens, 1, F32), shape(tokens, D, BF16)]
        + [shape(tokens, units, BF16), shape(tokens, units, F32)]
        + [shape(tokens, D, F32), shape(tokens, 1, F32)]
        + [jax.ShapeDtypeStruct((tokens // length, 1, D), F32)],
    )(normal_zero, context, share, vec, gathered, *[w_in] * pieces, *[w_out] * pieces)


def layer_back_kernel(pieces, *refs):
    grad_pooled, share, normal_two, scale_two, slope, normal_one, scale_one, vec, w_o = refs[:9]
    w_in, w_out = refs[9 : 9 + pieces], refs[9 + pieces : 9 + 2 * pieces]
    inner_ref, mixed_ref, attended_ref, context_ref, sums_ref = refs[9 + 2 * pieces :]
    grad_hidden = share[...] * grad_pooled[0]
    grad_two = normalize_back(grad_hidden, vec[12:13], normal_two[...], scale_two[...])
    branch = grad_two.astype(BF16)
    sums = []
    total = grad_two
    for part in range(pieces):
        columns = slice(part * D, (part + 1) * D)
        inner = (contract(branch, w_out[part][...], 1, 1) * slope[:, columns]).astype(BF16)
        inner_ref[:, columns] = inner
        sums.append(column_sum(inner.astype(F32)))
        total = total + contract(inner, w_in[part][...], 1, 1)
    mixed = normalize_back(total, vec[10:11], normal_one[...], scale_one[...])
    mixed_ref[...] = mixed
    attended = mixed.astype(BF16)
    attended_ref[...] = attended
    context_ref[...] = contract(attended, w_o[...], 1, 1).astype(BF16)
    sums += [
        column_sum(branch.astype(F32)),
        column_sum(total * normal_one[...]), column_sum(total),
        column_sum(grad_hidden * normal_two[...]), column_sum(grad_hidden),
        column_sum(attended.astype(F32)),
    ]
    sums += [jnp.zeros((1, D), F32)] * (sums_ref.shape[0] - len(sums))

    @pl.when(pl.program_id(0) == 0)
    def _():
        sums_ref[...] = jnp.zeros_like(sums_ref)

    sums_ref[...] += jnp.concatenate(sums, 0)


def layer_back(grad_pooled, share, normal_two, scale_two, slope, normal_one, scale_one, vec, gathered, w_in, w_out, length):
    tokens, units = slope.shape
    cycle, pieces = length // BLOCK, units // D
    return call(
        functools.partial(layer_back_kernel, pieces), "layer_back", (tokens // BLOCK,),
        [pl.BlockSpec((1, 1, D), lambda i: (i // cycle, 0, 0)), row_blocks(1), row_blocks(D), row_blocks(1)]
        + [row_blocks(units), row_blocks(D), row_blocks(1), fixed(vec.shape)]
        + weight_blocks(3, 1) + weight_blocks(0, pieces) + weight_row_blocks(pieces),
        [row_blocks(units), row_blocks(D), row_blocks(D), row_blocks(D), fixed((16, D))],
        [shape(tokens, units, BF16), shape(tokens, D, F32), shape(tokens, D, BF16)]
        + [shape(tokens, D, BF16), shape(16, D, F32)],
    )(grad_pooled, share, normal_two, scale_two, slope, normal_one, scale_one, vec, gathered, *[w_in] * pieces, *[w_out] * pieces)


def leave_kernel(place_rows, packed, mixed, normal, scale, vec, wq, wk, wv, low_ref, place_ref, sums_ref):
    total = mixed[...]
    for part, weight in enumerate((wq, wk, wv)):
        total = total + contract(packed[:, part * D : (part + 1) * D], weight[...], 1, 1)
    grad = normalize_back(total, vec[8:9], normal[...], scale[...])
    low_ref[...] = grad.astype(BF16)

    @pl.when(pl.program_id(1) == 0)
    def _():
        place_ref[...] = jnp.zeros_like(place_ref)

    places = place_rows
    for device in range(place_ref.shape[0]):
        place_ref[device, :places] += grad[device * places : (device + 1) * places]

    @pl.when((pl.program_id(0) == 0) & (pl.program_id(1) == 0))
    def _():
        sums_ref[...] = jnp.zeros_like(sums_ref)

    sums = [
        column_sum(total * normal[...]), column_sum(total),
        column_sum(packed[:, :D].astype(F32)), column_sum(packed[:, 2 * D :].astype(F32)),
        jnp.zeros((4, D), F32),
    ]
    sums_ref[...] += jnp.concatenate(sums, 0)


def leave(grad_packed, grad_mixed, normal, scale, vec, gathered, length, place_rows, rows):
    tokens = grad_mixed.shape[0]
    cycle = length // BLOCK
    blocks = lambda width: pl.BlockSpec((BLOCK, width), lambda j, s: (s * cycle + j, 0))
    place_block = pl.BlockSpec((BLOCK // place_rows, rows, D), lambda j, s: (j, 0, 0))
    still = lambda size, *index: pl.BlockSpec(size, lambda j, s: index, pipeline_mode=pl.Buffered(1))
    return call(
        functools.partial(leave_kernel, place_rows), "leave", (cycle, tokens // length),
        [blocks(3 * D), blocks(D), blocks(D), blocks(1), still(vec.shape, 0, 0)]
        + [still((D, D), 0, part) for part in range(3)],
        [blocks(D), place_block, still((8, D), 0, 0)],
        [shape(tokens, D, BF16), jax.ShapeDtypeStruct((length // place_rows, rows, D), F32), shape(8, D, F32)],
    )(grad_packed, grad_mixed, normal, scale, vec, *[gathered] * 3)


def weight_grad_kernel(counts, with_extra, core, *refs):
    pairs, (extra, kept_ref, sent_ref, total_ref) = refs[: 2 * len(counts)], refs[2 * len(counts) :]
    _, width, _, depth, rows, _ = kept_ref.shape
    groups = kept_ref.shape[0]
    step = pl.program_id(0)
    first = 0
    for index, count in enumerate(counts):
        left, right = pairs[2 * index : 2 * index + 2]

        @pl.when((step >= first) & (step < first + count))
        def _():
            total_ref[...] = contract(left[...], right[...], 0, 0)

        first += count

    def store(read):
        for own in range(2):

            @pl.when(core[0] == own)
            def _():
                for x in range(groups):
                    for z in range(depth):
                        for y in range(width):
                            kept_ref[x, y, 0, z] = read(x, own, z, y)
                            sent_ref[x, y, 0, z] = read(x, 1 - own, z, y).astype(BF16)

    @pl.when(step < first)
    def _():
        place = lambda x, side, z, y: (((2 * x + side) * depth + z) * width + y) * rows
        store(lambda *at: total_ref[place(*at) : place(*at) + rows, :])

    if with_extra:

        @pl.when(step == first)
        def _():
            store(lambda *at: extra[at])


def weight_grad(name, pairs, core, sizes, extra=None):
    tokens = pairs[0][0].shape[0]
    counts = [right.shape[1] // D for _, right in pairs]
    pieces = sum(counts) + (extra is not None)
    rows = D // (2 * sizes[0] * sizes[1] * sizes[2])
    extent = (sizes[0], sizes[2], pieces, sizes[1], rows, D)
    specs, first = [pl.BlockSpec(memory_space=pltpu.SMEM)], 0
    for count in counts:
        specs.append(pl.BlockSpec((tokens, D), lambda k: (0, 0)))
        specs.append(
            pl.BlockSpec(
                (tokens, D),
                functools.partial(lambda first, last, k: (0, jnp.clip(k - first, 0, last)), first, count - 1),
            )
        )
        first += count
    with_extra = extra is not None
    if not with_extra:
        extra = jnp.zeros((8, LANES), F32)
    specs.append(pl.BlockSpec(extra.shape, lambda k: (0,) * extra.ndim))
    out = pl.BlockSpec(extent[:2] + (1,) + extent[3:], lambda k: (0, 0, k, 0, 0, 0))
    return call(
        functools.partial(weight_grad_kernel, counts, with_extra), name, (pieces,), specs,
        [out, out],
        [jax.ShapeDtypeStruct(extent, F32), jax.ShapeDtypeStruct(extent, BF16)],
        scratch=[pltpu.VMEM((D, D), F32)],
    )(core, *[side for pair in pairs for side in pair], extra)


def outer_grad_kernel(core, left, grad_pooled, share, normal, scale, vec, kept_ref, sent_ref, branch):
    @pl.when((pl.program_id(0) == 0) & (pl.program_id(1) == 0))
    def _():
        sequences = grad_pooled.shape[0]
        length = share.shape[0] // sequences
        for index in range(sequences):
            part = slice(index * length, (index + 1) * length)
            grad_hidden = share[part] * grad_pooled[index]
            branch[part] = normalize_back(grad_hidden, vec[12:13], normal[part], scale[part]).astype(BF16)

    total = contract(left[...], branch[...], 0, 0)
    _, width, pieces, depth, rows, _ = kept_ref.shape

    def store(ref):
        for z in range(depth):
            for y in range(width):
                for piece in range(pieces):
                    first = ((z * width + y) * pieces + piece) * rows
                    ref[0, y, piece, z] = total[first : first + rows].astype(ref.dtype)

    @pl.when(pl.program_id(1) == 0)
    def _():
        store(kept_ref)

    @pl.when(pl.program_id(1) == 1)
    def _():
        store(sent_ref)


def outer_grad(left, grad_pooled, share, normal, scale, vec, core, sizes, rows):
    tokens, units = left.shape
    width = units // (2 * sizes[0])
    extent = (sizes[0], sizes[2], width // (sizes[1] * sizes[2] * rows), sizes[1], rows, D)
    out = pl.BlockSpec((1,) + extent[1:], lambda x, side, core: (x, 0, 0, 0, 0, 0))
    still = lambda values: pl.BlockSpec(values.shape, lambda x, side, core: (0,) * values.ndim)
    return pl.pallas_call(
        outer_grad_kernel,
        grid_spec=pltpu.PrefetchScalarGridSpec(
            num_scalar_prefetch=1,
            grid=(sizes[0], 2),
            in_specs=[
                pl.BlockSpec((tokens, width), lambda x, side, core: (0, 2 * x + (core[0] + side) % 2)),
                still(grad_pooled), still(share), still(normal), still(scale), still(vec),
            ],
            out_specs=[out, out],
            scratch_shapes=[pltpu.VMEM((tokens, D), BF16)],
        ),
        out_shape=[jax.ShapeDtypeStruct(extent, F32), jax.ShapeDtypeStruct(extent, BF16)],
        cost_estimate=CHEAP,
        compiler_params=pltpu.CompilerParams(vmem_limit_bytes=36 * MIB),
        name="grad_outer",
    )(core, left, grad_pooled, share, normal, scale, vec)


def split_kernel(count, partners, *refs):
    inputs, outputs = refs[:count], refs[count:]
    for index, out in enumerate(outputs):
        part = partners[index]
        total = inputs[0][part, 0].astype(F32)
        for more in inputs[1:]:
            total = total + more[part, 0].astype(F32)
        out[0] = total.astype(out.dtype)


def split(name, values, partners):
    parts, pieces = values[0].shape[:2]
    rest = values[0].shape[2:]
    zeros = (0,) * len(rest)
    return call(
        functools.partial(split_kernel, len(values)), name, (pieces,),
        [pl.BlockSpec(memory_space=pltpu.SMEM)]
        + [pl.BlockSpec((parts, 1) + rest, lambda k: (0, k) + zeros)] * len(values),
        [pl.BlockSpec((1,) + rest, lambda k: (k,) + zeros)] * parts,
        [jax.ShapeDtypeStruct((pieces,) + rest, F32 if part == 0 else BF16) for part in range(parts)],
    )(partners, *values)


def fold_kernel(count, partners, *refs):
    inputs, outputs = refs[:count], refs[count:]
    for index, out in enumerate(outputs):
        part = partners[index]
        total = inputs[0][0, part]
        for more in inputs[1:]:
            total = total + more[0, part].astype(F32)
        out[0] = total.astype(out.dtype)


def fold(name, values, partners):
    pieces, parts, rows, _ = values[0].shape
    return call(
        functools.partial(fold_kernel, len(values)), name, (pieces,),
        [pl.BlockSpec(memory_space=pltpu.SMEM)]
        + [pl.BlockSpec((1, parts, rows, D), lambda k: (k, 0, 0, 0))] * len(values),
        [pl.BlockSpec((1, rows, D), lambda k: (k, 0, 0))] * parts,
        [jax.ShapeDtypeStruct((pieces, rows, D), F32 if part == 0 else BF16) for part in range(parts)],
    )(partners, *values)


def assemble_kernel(sources, width, counts, core, in_plane, *refs):
    inputs, outputs = refs[: -len(counts)], refs[-len(counts) :]
    for index in range(2 * sources):
        side = core[0] if index < sources else 1 - core[0]
        plane = in_plane[index % sources]
        x, y = plane // width, plane % width
        for place, out_ref in enumerate(outputs):
            ref = inputs[index * len(outputs) + place]
            for step in range(ref.shape[0]):
                if len(out_ref.shape) == 6:
                    out_ref[x, side, step, y] = ref[step, 0]
                else:
                    out_ref[x, side, step, y, 0] = ref[step, 0]


def assemble(name, own, came, core, in_plane, sizes, wide, tall=0):
    depth, _, rows, _ = own[0].shape
    smem = pl.BlockSpec(memory_space=pltpu.SMEM)
    block = lambda first: pl.BlockSpec((depth, 1, rows, D), lambda k: (0, first + k, 0, 0))
    extent = (sizes[0], 2, depth, sizes[2])
    outs = [pl.BlockSpec(extent + (rows, D), lambda k: (0, 0, 0, 0, 0, k))]
    shapes = [jax.ShapeDtypeStruct(extent + (rows, wide * D), BF16)]
    if tall:
        outs.append(pl.BlockSpec(extent + (1, rows, D), lambda k: (0, 0, 0, 0, k, 0, 0)))
        shapes.append(jax.ShapeDtypeStruct(extent + (tall, rows, D), BF16))
    parts = (*own, *came)
    firsts = (0, wide)[: len(outs)]
    made = call(
        functools.partial(assemble_kernel, len(own), sizes[2], (wide, tall)[: len(outs)]), name, (wide,),
        [smem, smem] + [block(first) for _ in parts for first in firsts],
        outs, shapes,
    )(core, in_plane, *[part for part in parts for _ in firsts])
    return [made[0].reshape(D, -1)] + [part.reshape(-1, D) for part in made[1:]]


def give_kernel(room, slot, grad, vectors, out_ref):
    first = pl.program_id(0) * out_ref.shape[0]
    rows = first + lax.broadcasted_iota(jnp.int32, (out_ref.shape[0], slot.shape[1]), 0)
    total = matmul(jnp.where(rows == slot[...], 1.0, 0.0).astype(BF16), grad[...])
    devices = vectors.shape[0]
    rows = first + lax.broadcasted_iota(jnp.int32, (out_ref.shape[0], devices), 0)
    last = lax.broadcasted_iota(jnp.int32, (out_ref.shape[0], devices), 1) * room + room - 1
    total = total + matmul(jnp.where(rows == last, 1.0, 0.0).astype(BF16), vectors[...])
    out_ref[...] = total.astype(BF16)


def give_rows(slot, grad, vectors, room):
    devices = vectors.shape[0]
    block = 8 * room
    return call(
        functools.partial(give_kernel, room), "give", (devices // 8,),
        [fixed(slot.shape), fixed(grad.shape), fixed(vectors.shape)],
        pl.BlockSpec((block, D), lambda i: (i, 0)),
        shape(devices * room, D, BF16),
    )(slot, grad, vectors)


PARTS = 2


def head_marks():
    half = lax.broadcasted_iota(jnp.int32, (1, LANES), 1) // HEAD_DIM
    return [jnp.where(half == head, 1.0, 0.0).astype(BF16) for head in range(2)]


def attend_kernel(mask_ref, q_ref, k_ref, v_ref, ctx_ref, lse_ref):
    keep = mask_ref[0] > 0
    lane = lax.broadcasted_iota(jnp.int32, (1, LANES), 1)
    scale = jnp.asarray(HEAD_DIM ** (-0.5), BF16)
    log_total = jnp.zeros(lse_ref.shape[1:], F32)
    for pair in range(q_ref.shape[1] // LANES):
        columns = slice(pair * LANES, (pair + 1) * LANES)
        queries, keys, values = q_ref[:, columns], k_ref[:, columns], v_ref[:, columns]
        context = jnp.zeros(queries.shape, F32)
        for head, own in enumerate(head_marks()):
            scores = contract(queries, keys * (own * scale), 1, 1)
            scores = jnp.where(keep, scores, -1000000000.0)
            peak = jnp.max(scores, 1, keepdims=True)
            exponent = jnp.exp(scores - peak)
            total = jnp.sum(exponent, 1, keepdims=True)
            weights = (exponent * (1.0 / total)).astype(BF16)
            context = context + matmul(weights, values * own)
            log_total = jnp.where(lane == 2 * pair + head, peak + jnp.log(total), log_total)
        ctx_ref[:, columns] = context.astype(BF16)
    lse_ref[0] = log_total


def attend_back_kernel(mask_ref, q_ref, k_ref, v_ref, dctx_ref, lse_ref, grad_ref):
    keep = mask_ref[0] > 0
    scale = HEAD_DIM ** (-0.5)
    width = q_ref.shape[1]
    for pair in range(width // LANES):
        columns = slice(pair * LANES, (pair + 1) * LANES)
        queries, keys, values, dctx = (ref[:, columns] for ref in (q_ref, k_ref, v_ref, dctx_ref))
        grad_q, grad_k, grad_v = (jnp.zeros(queries.shape, F32) for _ in range(3))
        for head, own in enumerate(head_marks()):
            own_keys = keys * (own * jnp.asarray(scale, BF16))
            own_dctx = dctx * own
            scores = contract(queries, own_keys, 1, 1)
            scores = jnp.where(keep, scores, -1000000000.0)
            spot = 2 * pair + head
            weights = jnp.exp(scores - lse_ref[0, :, spot : spot + 1])
            grad_weights = contract(own_dctx, values, 1, 1)
            inner = jnp.sum(grad_weights * weights, 1, keepdims=True)
            grad_scores = (weights * (grad_weights - inner)).astype(BF16)
            grad_q = grad_q + matmul(grad_scores, own_keys)
            grad_k = grad_k + contract(grad_scores, queries * own, 0, 0)
            grad_v = grad_v + contract(weights.astype(BF16), own_dctx, 0, 0)
        for part, grad in enumerate((grad_q, grad_k * scale, grad_v)):
            start = pl.multiple_of(part * D + pl.program_id(1) * width + pair * LANES, LANES)
            grad_ref[:, pl.ds(start, LANES)] = grad.astype(BF16)


def attend_specs(length):
    width = D // PARTS
    block = lambda part: pl.BlockSpec((length, width), lambda s, h: (s, part * PARTS + h))
    mask = pl.BlockSpec((1, 1, length), lambda s, h: (s, 0, 0))
    sums = pl.BlockSpec((1, length, LANES), lambda s, h: (h, s, 0))
    return [mask, block(0), block(1), block(2)], block(0), sums


def attend(packed, mask, sequences, length):
    tokens = sequences * length
    inputs, plain, sums = attend_specs(length)
    return call(
        attend_kernel, "attend", (sequences, PARTS), inputs, [plain, sums],
        [shape(tokens, D, BF16), jax.ShapeDtypeStruct((PARTS, tokens, LANES), F32)],
    )(mask, packed, packed, packed)


def attend_back(packed, mask, grad_context, log_total, sequences, length):
    inputs, plain, sums = attend_specs(length)
    return call(
        attend_back_kernel, "attend_back", (sequences, PARTS), inputs + [plain, sums],
        pl.BlockSpec((length, 3 * D), lambda s, h: (s, 0)),
        shape(sequences * length, 3 * D, BF16),
    )(mask, packed, packed, packed, grad_context, log_total)


def unit(values):
    scale = lax.rsqrt(jnp.sum(values * values, -1, keepdims=True) + NORM_EPSILON)
    return values * scale, scale


def loss_kernel(me, q_ref, p_ref, source_ref, positive_ref, loss_ref, grad_ref, all_ref):
    queries, query_scale = unit(q_ref[...])
    passages, passage_scale = unit(p_ref[...])
    count = queries.shape[0]
    precise = lax.Precision.HIGHEST
    feature = lax.broadcasted_iota(jnp.int32, (1, D), 1)
    chosen = lax.broadcasted_iota(jnp.int32, (count, count), 1) == positive_ref[...]
    source = source_ref[...]
    own_source = jnp.sum(jnp.where(chosen, source, 0), 1, keepdims=True)
    keeping = source == own_source
    loss = jnp.zeros((1, 1), F32)
    grad_q = jnp.zeros_like(queries)
    grad_p = jnp.zeros_like(passages)
    for width in WIDTHS:
        inside = feature < width
        left, left_scale = unit(jnp.where(inside, queries, 0.0))
        right, right_scale = unit(jnp.where(inside, passages, 0.0))
        scores = contract(left, right, 1, 1, precise) / TEMPER
        scores = jnp.where(keeping, scores, -1000000000.0)
        peak = jnp.max(scores, 1, keepdims=True)
        exponent = jnp.exp(scores - peak)
        total = jnp.sum(exponent, 1, keepdims=True)
        target = jnp.sum(jnp.where(chosen, scores, 0.0), 1, keepdims=True)
        loss = loss + jnp.sum(peak + jnp.log(total) - target, 0, keepdims=True)
        slope = jnp.where(keeping, exponent / total - jnp.where(chosen, 1.0, 0.0), 0.0)
        slope = slope * (1.0 / (TEMPER * count))
        grad_left = contract(slope, right, 1, 0, precise)
        grad_right = contract(slope, left, 0, 0, precise)
        grad_q = grad_q + left_scale * (
            grad_left - left * jnp.sum(grad_left * left, -1, keepdims=True)
        )
        grad_p = grad_p + right_scale * (
            grad_right - right * jnp.sum(grad_right * right, -1, keepdims=True)
        )
    loss_ref[...] = loss / count
    own = grad_ref.shape[0] // 2
    for side, (grad, values, scale) in enumerate(
        ((grad_q, queries, query_scale), (grad_p, passages, passage_scale))
    ):
        all_ref[side] = scale * (grad - values * jnp.sum(grad * values, -1, keepdims=True))
        for row in range(own):
            grad_ref[side * own + row] = all_ref[side, pl.ds(me[0] * own + row, 1), :]


def loss_and_grads(queries, passages, source, positive, me, own):
    count = queries.shape[0]
    vmem = pl.BlockSpec(memory_space=pltpu.VMEM)
    return pl.pallas_call(
        loss_kernel,
        in_specs=[pl.BlockSpec(memory_space=pltpu.SMEM)] + [vmem] * 4,
        out_shape=[
            jax.ShapeDtypeStruct((1, 1), F32),
            jax.ShapeDtypeStruct((2 * own, 1, D), F32),
        ],
        scratch_shapes=[pltpu.VMEM((2, count, D), F32)],
        cost_estimate=CHEAP,
        compiler_params=pltpu.CompilerParams(vmem_limit_bytes=32 * MIB),
        name="loss",
    )(me[None], queries, passages, source.reshape(1, count), positive.reshape(count, 1))


def everyone(values):
    devices = lax.axis_size(AXES)
    copies = jnp.broadcast_to(values[None], (devices,) + values.shape)
    return lax.all_to_all(copies, AXES, 0, 0, tiled=True)


def other_core(values):
    return lax.ppermute(values, "core", [(0, 1), (1, 0)])


def tie(anchor, *values):
    return lax.optimization_barrier((anchor,) + values)


PLANE = ("x", "y")


def partner(index, shift, count):
    return (index + shift) % count if count & (count - 1) else index ^ shift


def partners_of(axes):
    count, me = lax.axis_size(axes), lax.axis_index(axes).astype(jnp.int32)
    return jnp.stack([jnp.int32(0) + partner(me, shift, count) for shift in range(count)])


def spread(values, axes):
    count = lax.axis_size(axes)
    return [values] + [
        lax.ppermute(values, axes, [(i, partner(i, shift, count)) for i in range(count)])
        for shift in range(1, count)
    ]


def trade(parts, axes):
    count = lax.axis_size(axes)
    return [parts[0]] + [
        lax.ppermute(parts[shift], axes, [(i, partner(i, shift, count)) for i in range(count)])
        for shift in range(1, count)
    ]


def finish_kernel(counts, table_squares, *refs):
    inputs, outputs = refs[: sum(counts)], refs[sum(counts) :]
    place_ref, qkv_ref, proj_ref, inner_ref, outer_ref, squares_ref = outputs
    totals, first = [], 0
    for count in counts:
        total = inputs[first][...]
        for more in inputs[first + 1 : first + count]:
            total = total + more[...].astype(F32)
        totals.append(total)
        first += count
    outer, inner, packed = totals
    pieces, rows = outer.shape[:2]
    squares = table_squares[...]
    for piece in range(pieces):
        outer_ref[piece * rows : (piece + 1) * rows] = outer[piece]
        inner_ref[:, piece * D : (piece + 1) * D] = inner[piece]
    for piece in range(3):
        qkv_ref[:, piece * D : (piece + 1) * D] = packed[piece]
    proj_ref[...] = inner[pieces]
    place_ref[...] = packed[3, : place_ref.shape[0]]
    for total in totals:
        squares = squares + jnp.sum(jnp.sum(total * total, 0), keepdims=True)
    squares_ref[...] = jnp.broadcast_to(squares[None], squares_ref.shape)


def finish(table_squares, outer, inner, packed, place_rows, devices):
    pieces, rows = outer[0].shape[:2]
    parts = (outer, inner, packed)
    return pl.pallas_call(
        functools.partial(finish_kernel, [len(part) for part in parts]),
        out_shape=[
            shape(place_rows, D, F32), shape(rows, 3 * D, F32), shape(rows, D, F32),
            shape(rows, pieces * D, F32), shape(pieces * rows, D, F32),
            jax.ShapeDtypeStruct((devices, 1, LANES), F32),
        ],
        cost_estimate=CHEAP,
        compiler_params=pltpu.CompilerParams(vmem_limit_bytes=60 * MIB),
        name="finish",
    )(table_squares, *outer, *inner, *packed)


def update_kernel(squares, *refs):
    count = 7
    gradients, masters, firsts, seconds = (refs[part * count : (part + 1) * count] for part in range(4))
    outputs, norm_ref = refs[4 * count : 7 * count], refs[7 * count]
    norm = jnp.sqrt(jnp.sum(squares[...][:, 0, :1], 0, keepdims=True))
    factor = jnp.minimum(1.0, CLIP_LIMIT / (norm + 1e-06))
    norm_ref[...] = norm

    def update(index):
        rate, decay = (VECTOR_RATE, 0.0) if index == count - 1 else (LEARN_RATE, WEIGHT_DECAY)
        clipped = gradients[index][...] * factor
        first = BETA_FIRST * firsts[index][...] + (1.0 - BETA_FIRST) * clipped
        second = BETA_SECOND * seconds[index][...] + (1.0 - BETA_SECOND) * clipped * clipped
        ratio = (
            first
            * (1.0 / (1.0 - BETA_FIRST**STEP))
            / (jnp.sqrt(second * (1.0 / (1.0 - BETA_SECOND**STEP))) + EPSILON)
        )
        master = masters[index][...]
        outputs[index][...] = master - rate * (ratio + decay * master)
        outputs[count + index][...] = first
        outputs[2 * count + index][...] = second

    update(0)

    @pl.when(pl.program_id(0) == 0)
    def _():
        for index in range(1, count):
            update(index)


def update_all(squares, gradients, masters, firsts, seconds):
    owned = masters[0].shape[0]
    block = max(size for size in range(8, 241, 8) if owned % size == 0)
    specs = [pl.BlockSpec((block, D), lambda i: (i, 0))]
    specs += [fixed(master.shape) for master in masters[1:]]
    return call(
        update_kernel, "update", (owned // block,),
        [fixed(squares.shape)] + specs * 4,
        specs * 3 + [fixed((1, 1))],
        [jax.ShapeDtypeStruct(master.shape, F32) for master in masters] * 3 + [shape(1, 1, F32)],
    )(squares, *gradients, *masters, *firsts, *seconds)


def per_device(query_ids, query_mask, passage_ids, passage_mask, source, positive, *weights):
    masters, firsts, seconds = weights[:7], weights[7:14], weights[14:]
    table, positions, w_qkv, w_o, w_in, w_out, vectors = masters
    sizes = tuple(lax.axis_size(name) for name in AXES)
    devices = lax.axis_size(AXES)
    pair_rows, length = query_ids.shape
    sequences = 2 * pair_rows
    tokens = sequences * length
    owned, rows = table.shape[0], w_qkv.shape[0]
    me = lax.axis_index(AXES)

    place_rows = positions.shape[0]
    vector_size = vectors.shape[0] * vectors.shape[1]
    vector_rows_used = -(-vector_size // D)
    vector_flat = jnp.pad(vectors.reshape(-1), (0, vector_rows_used * D - vector_size))
    units = w_in.shape[1]
    pieces = units // D
    core = lax.axis_index("core").astype(jnp.int32)[None]
    extents = (sizes[0],) + sizes[2:]
    in_plane, in_depth = partners_of(PLANE), partners_of("z")
    own_pieces = pieces_of(
        w_qkv, w_o, positions, vector_flat.reshape(vector_rows_used, D), w_in, w_out
    )
    column = lax.all_gather(own_pieces, "z", axis=0, tiled=True).reshape((sizes[2],) + own_pieces.shape)

    room = min(LANES - 1, max(16, round_up(5 * tokens // (4 * devices), 8)))
    query_ids, _ = tie(query_ids, own_pieces)
    slot_column, slot_row, rank, fresh, wants = plan_of(query_ids, passage_ids, owned, room, devices)
    swap = lambda values: lax.all_to_all(values, AXES, 0, 0, tiled=True)
    token_mask = jnp.concatenate([query_mask, passage_mask]).astype(F32)
    mask_row = token_mask[:, None, :]
    share = (token_mask / jnp.sum(token_mask, 1, keepdims=True)).reshape(tokens, 1)
    asked = swap(wants)
    zeros = jnp.zeros((tokens, D), F32)
    asked, mask_row, share, zeros = tie(asked, mask_row, share, zeros)
    chosen, found = lookup(asked, table, room)
    column, _ = tie(column, found)
    found = swap(found)
    plane = spread(column[:, :5], PLANE)
    pair_plane = spread(column[:, 5:], PLANE)
    plane_other = [other_core(part) for part in plane]
    (gathered,) = assemble("assemble", plane, plane_other, core, in_plane, extents, 5)

    turns = jnp.max(asked[:, LANES - 1]) // (room - 1) + 1
    slots = jnp.arange(devices * room, dtype=jnp.int32)
    ids = jnp.concatenate([query_ids, passage_ids]).reshape(-1)

    def turn_of(turn):
        spot = rank[0] - turn * (room - 1)
        slot = jnp.where((spot >= 0) & (spot < room - 1), ids // owned * room + spot, -1)
        match = (slots[:, None] == slot[None, :]) & (fresh > 0)
        wants = jnp.sum(jnp.where(match, ids % owned + 1, 0), 1).reshape(devices, room)
        return slot, swap(jnp.pad(wants, ((0, 0), (0, LANES - room))))

    def fetch_more(state):
        turn, values = state
        slot, asked = turn_of(turn)
        found = swap(lookup(asked, table, room)[1])
        return turn + 1, values + matmul((slot[:, None] == slots[None, :]).astype(BF16), found)

    _, looked_up = lax.while_loop(
        lambda state: state[0] < turns, fetch_more, (jnp.int32(1), zeros)
    )

    vec = vec_of(gathered, vectors.shape[0], vectors.shape[1], place_rows, rows)
    normal_zero, scale_zero, low_zero, packed = enter(
        slot_column, found, looked_up, vec, gathered, length, place_rows, rows
    )
    context, log_total = attend(packed, mask_row, sequences, length)
    context, *pair_plane = tie(context, *pair_plane)
    pair_other = [other_core(part) for part in pair_plane]
    inner_full, outer_full = assemble(
        "assemble_pair", pair_plane, pair_other, core, in_plane, extents, pieces, pieces
    )
    normal_one, scale_one, low_one, activated, slope, normal_two, scale_two, pooled = layer(
        normal_zero, context, share, vec, gathered, inner_full, outer_full, length
    )

    shared = everyone(pooled[:, 0]).reshape(devices, 2, pair_rows, D)
    loss, grad_pooled = loss_and_grads(
        shared[:, 0].reshape(-1, D), shared[:, 1].reshape(-1, D), source, positive,
        me.astype(jnp.int32), pair_rows,
    )

    by_plane = lambda values: values.reshape((-1,) + values.shape[2:])
    outer_kept, outer_sent = outer_grad(
        activated, grad_pooled, share, normal_two, scale_two, vec, core, extents, rows
    )
    outer_came = other_core(outer_sent)
    outer_parts = split("split_outer", [by_plane(outer_kept), by_plane(outer_came)], in_plane)
    outer_plane = trade(outer_parts, PLANE)
    slope, *_ = tie(slope, *outer_parts)
    grad_inner, grad_mixed, attended, grad_context, sums = layer_back(
        grad_pooled, share, normal_two, scale_two, slope, normal_one, scale_one, vec,
        gathered, inner_full, outer_full, length,
    )
    grad_inner, attended, *outer_plane = tie(grad_inner, attended, *outer_plane)
    outer_parts = fold("fold_outer", outer_plane, in_depth)
    outer_depth = trade(outer_parts, "z")
    grad_inner, attended, *_ = tie(grad_inner, attended, *outer_parts)
    inner_kept, inner_sent = weight_grad(
        "grad_inner", [(low_one, grad_inner), (context, attended)], core, extents
    )
    inner_kept, inner_sent, *outer_depth = tie(inner_kept, inner_sent, *outer_depth)
    inner_came = other_core(inner_sent)
    inner_parts = split("split_inner", [by_plane(inner_kept), by_plane(inner_came)], in_plane)
    inner_plane = trade(inner_parts, PLANE)
    grad_context, *_ = tie(grad_context, *inner_parts)
    grad_packed = attend_back(packed, mask_row, grad_context, log_total, sequences, length)
    grad_packed, *inner_plane = tie(grad_packed, *inner_plane)
    inner_parts = fold("fold_inner", inner_plane, in_depth)
    grad_packed, *inner_parts = tie(grad_packed, *inner_parts)
    inner_depth = trade(inner_parts, "z")
    low_input, grad_position, end_sums = leave(
        grad_packed, grad_mixed, normal_zero, scale_zero, vec, gathered, length, place_rows, rows
    )
    low_input, grad_position, end_sums, *inner_depth = tie(
        low_input, grad_position, end_sums, *inner_depth
    )

    grad_vectors = jnp.concatenate(
        [end_sums[2:4], sums[pieces + 5 : pieces + 6], sums[:pieces]]
        + [sums[pieces : pieces + 1], end_sums[:2], sums[pieces + 1 : pieces + 5]]
    )
    vector_pieces = grad_vectors.reshape(-1, devices, vectors.shape[1]).transpose(1, 0, 2)
    vector_pieces = vector_pieces.reshape(devices, -1)
    vector_high = lax.reduce_precision(vector_pieces, 8, 7)
    vector_pieces = jnp.concatenate([vector_high, vector_pieces - vector_high], 1)
    vector_pieces = jnp.pad(vector_pieces, ((0, 0), (0, D - 2 * vector_size))).astype(BF16)

    def give_more(state):
        turn, values = state
        slot, asked = turn_of(turn)
        given = swap(give_rows(slot[None], low_input, jnp.zeros_like(vector_pieces), room))
        return turn + 1, values + take_rows(lookup(asked, table, room)[0], given)

    summed = give_rows(slot_row, low_input, vector_pieces, room)
    given = swap(summed)
    low_zero, _ = tie(low_zero, summed)

    grad_position = jnp.pad(grad_position, ((0, devices - grad_position.shape[0]), (0, 0), (0, 0)))
    grad_position = grad_position.reshape(sizes + (rows, D))
    packed_kept, packed_sent = weight_grad(
        "grad_packed", [(low_zero, grad_packed)], core, extents, grad_position
    )
    packed_came = other_core(packed_sent)
    packed_plane = trade(split("split_packed", [by_plane(packed_kept), by_plane(packed_came)], in_plane), PLANE)
    _, table_grad = lax.while_loop(
        lambda state: state[0] < turns, give_more, (jnp.int32(1), take_rows(chosen, given))
    )
    sum_vectors = jnp.sum(
        given.reshape(devices, room, D)[:, room - 1, : 2 * vector_size].astype(F32), 0
    )
    sum_vectors = (sum_vectors[:vector_size] + sum_vectors[vector_size:]).reshape(vectors.shape)
    squares = jnp.sum(table_grad * table_grad) + jnp.sum(sum_vectors * sum_vectors)
    squares, *packed_plane = tie(squares, *packed_plane)
    packed_depth = trade(fold("fold_packed", packed_plane, in_depth), "z")
    *small_grads, squares = finish(
        squares.reshape(1, 1), outer_depth, inner_depth, packed_depth, place_rows, devices
    )
    squares = lax.all_to_all(squares, AXES, 0, 0, tiled=True)
    *new, grad_norm = update_all(
        squares, (table_grad, *small_grads, sum_vectors), masters, firsts, seconds
    )
    return (*new, loss[0, 0], grad_norm[0, 0])


def solution(mesh):
    outer, dp = mesh.shape["outer"], mesh.shape["dp"]
    x = outer // 2
    y = x if dp % x == 0 else 1
    fine = Mesh(np.asarray(mesh.devices).reshape(x, 2, dp // y, y), AXES)
    by_row, by_column, whole = P(AXES, None), P(None, AXES), P()
    seven = (by_row,) * 6 + (by_column,)
    return jax.shard_map(
        per_device,
        mesh=fine,
        in_specs=(by_row,) * 4 + (whole,) * 2 + seven * 3,
        out_specs=seven * 3 + (whole, whole),
        check_vma=False,
    )
```
